768 devices in a mesh: wide: 32 (over z_hi, x, core), narrow: 24 (over y, z_lo).
Axes of the slice: x: 4, y: 8, z: 12 (z_hi: 4, z_lo: 3; z = z_hi * 3 + z_lo), core: 2. Of those that a mesh axis runs over, the one named last changes fastest.
Arguments:
- picture_vectors: bfloat16 [24576, 1152], P('wide')
- sentence_vectors: bfloat16 [24576, 1152], P('wide')
- matched_text_indices: int32 [24576], P('wide'), may hold values from 0 to 24575, as said below
- partner_table: int32 [5, 32], replicated, may hold values from 0 to 31, as said below
- trained_steepness: float32 [1], replicated, may hold values from 60 to 120
- learned_shift: float32 [1], replicated, may hold values from -6 to -3
Outputs:
- photo_slopes: float32 [24576, 1152], P(('wide', 'narrow'))
- wording_slopes: float32 [24576, 1152], P(('wide', 'narrow'))
The draws below stay inside these ranges and needn't reach their ends.
Inputs may be any that keep to these rules, and one draw needn't show every extreme that they name: `matched_text_indices`: every image's matching text lies in the image's own block of 768 consecutive rows, and every text is matched by exactly one image. Each row r is a perfect matching of the blocks of the form partner_table[r, i] = i XOR m_r, with round masks m_r that differ between rounds and are never 0.
All inputs are finite; a program needn't handle non-finite values.
Results may differ from the reference program's by a relative error of at most 0.0018.
Values may be sent and summed in bfloat16 or wider, within the bound.
No kernel may reach another device: no remote copies, remote signals or barrier semaphores. Data moves between devices by JAX's collectives and lax.ppermute only.
A program may use at most 64 MiB of HBM per device.

```python
import math
import jax
import jax.numpy as jnp
from jax import lax

CODE_SPAN = 1152
ROWS = 768
ROUNDS = 5
TOKENS = 24576
N_WIDE = 32


def draw_picture_vectors(key, part):
    key = jax.random.fold_in(key, 11)
    return jax.random.truncated_normal(key, -6.0, 6.0, (TOKENS, CODE_SPAN), jnp.float32).astype(jnp.bfloat16)


def draw_sentence_vectors(key, part):
    key = jax.random.fold_in(key, 13)
    return jax.random.truncated_normal(key, -6.0, 6.0, (TOKENS, CODE_SPAN), jnp.float32).astype(jnp.bfloat16)


def block_order(block_key):
    return jax.random.permutation(block_key, ROWS)


def draw_matched_text_indices(key, part):
    key = jax.random.fold_in(key, 5)
    block_keys = jax.random.split(key, N_WIDE)
    orders = jax.vmap(block_order)(block_keys).astype(jnp.int32)
    offsets = jnp.arange(N_WIDE, dtype=jnp.int32)[:, None] * ROWS
    return (orders + offsets).reshape(TOKENS)


def draw_partner_table(key, part):
    key = jax.random.fold_in(key, 7)
    round_masks = jax.random.permutation(key, N_WIDE - 1)[:ROUNDS].astype(jnp.int32) + 1
    block_ids = jnp.arange(N_WIDE, dtype=jnp.int32)
    return jnp.bitwise_xor(block_ids[None, :], round_masks[:, None])


def setup_inputs(seed: int = 0) -> dict:
    key_list = jax.random.split(jax.random.key(seed), 7)
    picture_vectors = draw_picture_vectors(jax.random.fold_in(key_list[6], 71), 0)
    sentence_vectors = draw_sentence_vectors(jax.random.fold_in(key_list[6], 71), 0)
    matched_text_indices = draw_matched_text_indices(jax.random.fold_in(key_list[6], 71), 0)
    partner_table = draw_partner_table(jax.random.fold_in(key_list[6], 71), 0)
    trained_steepness = jnp.clip(jnp.exp(jax.random.uniform(key_list[4], (1,), jnp.float32, math.log(60.0), math.log(120.0))), 60.0, 120.0)
    learned_shift = jnp.clip(jax.random.uniform(key_list[5], (1,), jnp.float32, -6.0, -3.0), -6.0, -3.0)
    return {"picture_vectors": picture_vectors, "sentence_vectors": sentence_vectors, "matched_text_indices": matched_text_indices, "partner_table": partner_table, "trained_steepness": trained_steepness, "learned_shift": learned_shift}


def patch_penalty_parts(photo_groups, wording_groups, diagonal_groups, opponent_numbers, sharpening_coefficient, starting_point):
    inner_results = jnp.einsum("nid,njd->nij", photo_groups.astype(jnp.float32), wording_groups.astype(jnp.float32))
    raw_similarity = sharpening_coefficient * inner_results + starting_point
    columns = opponent_numbers[:, None, None] * ROWS + jnp.arange(ROWS, dtype=jnp.int32)[None, None, :]
    plus_minus_grid = jnp.where(diagonal_groups[:, :, None] == columns, 1.0, -1.0).astype(jnp.float32)
    nearest_whole = lax.optimization_barrier((-sharpening_coefficient * plus_minus_grid * jax.nn.sigmoid(-plus_minus_grid * raw_similarity)).astype(jnp.bfloat16))
    weights = nearest_whole.astype(jnp.float32)
    photo_slope = jnp.einsum("nij,njd->nid", weights, wording_groups.astype(jnp.float32))
    wording_slope = jnp.einsum("nij,nid->njd", weights, photo_groups.astype(jnp.float32))
    return photo_slope, wording_slope


def reference(picture_vectors, sentence_vectors, matched_text_indices, partner_table, trained_steepness, learned_shift):
    blocks = N_WIDE
    photo_groups = picture_vectors.reshape(blocks, ROWS, CODE_SPAN)
    wording_groups = sentence_vectors.reshape(blocks, ROWS, CODE_SPAN)
    diagonal_groups = matched_text_indices.reshape(blocks, ROWS)
    sharpening_coefficient = trained_steepness[0] / CODE_SPAN
    starting_point = learned_shift[0]
    home_numbers = jnp.arange(blocks, dtype=jnp.int32)
    photo_slopes, wording_slopes = patch_penalty_parts(photo_groups, wording_groups, diagonal_groups, home_numbers, sharpening_coefficient, starting_point)
    for round_index in range(ROUNDS):
        opponent_numbers = partner_table[round_index].astype(jnp.int32)
        photo_slope, wording_slope = patch_penalty_parts(photo_groups, wording_groups[opponent_numbers], diagonal_groups, opponent_numbers, sharpening_coefficient, starting_point)
        photo_slopes = photo_slopes + photo_slope
        wording_slopes = wording_slopes.at[opponent_numbers].add(wording_slope)
    return photo_slopes.reshape(TOKENS, CODE_SPAN), wording_slopes.reshape(TOKENS, CODE_SPAN)
```

```python
import functools
import jax
import jax.numpy as jnp
import numpy as np
from jax import lax
from jax.sharding import PartitionSpec as P

WIDE = 32
Z_GROUPS = 4


def permute(array, pairs):
    return lax.ppermute(array, "wide", pairs)


def xor_pairs(mask):
    return [(i, i ^ mask) for i in range(WIDE)]


def z_pairs(step):
    return [(i, (i + 8 * step) % WIDE) for i in range(WIDE)]


def splits(rounds):
    return [
        (first, second, third)
        for first in range(rounds + 1)
        for second in range(rounds + 1 - first)
        for third in range(rounds + 1 - first - second)
    ]


def move_along_x(counts, rounds, stack):
    pieces = []
    start = rounds - sum(counts)
    if start:
        pieces.append(stack[:start])
    moved = {}
    offsets = {}
    for mask, count in enumerate(counts, 1):
        offsets[mask] = (start, count)
        start += count
    for mask in (2, 1, 3):
        begin, count = offsets[mask]
        if count:
            moved[mask] = permute(stack[begin : begin + count], xor_pairs(2 * mask))
    pieces += [moved[mask] for mask in sorted(moved)]
    return jnp.concatenate(pieces, axis=0) if len(pieces) > 1 else pieces[0]


def dot_last(left, right):
    return lax.dot_general(left, right, (((1,), (1,)), ((), ())), preferred_element_type=jnp.float32)


def dot(left, right):
    return jnp.dot(left, right, preferred_element_type=jnp.float32)


def local(
    picture_vectors,
    sentence_vectors,
    matched_text_indices,
    partner_table,
    trained_steepness,
    learned_shift,
):
    rows, span = picture_vectors.shape
    rounds = partner_table.shape[0]
    share = rows // lax.axis_size("narrow")
    myself = lax.axis_index("wide")
    begin = lax.axis_index("narrow") * share
    scale = trained_steepness[0] / span
    shift = learned_shift[0]
    my_z = myself // 8

    pictures = lax.dynamic_slice_in_dim(picture_vectors, begin, share, 0)
    texts = lax.dynamic_slice_in_dim(sentence_vectors, begin, share, 0)

    below_pictures = permute(pictures, z_pairs(1))
    above_texts = permute(texts, z_pairs(-1))
    below_texts = permute(texts, z_pairs(1))
    above_pictures = permute(pictures, z_pairs(-1))
    across_pictures = permute(below_pictures, z_pairs(1))
    across_texts = permute(above_texts, z_pairs(-1))
    other_pictures = permute(picture_vectors, xor_pairs(1))
    other_texts = permute(sentence_vectors, xor_pairs(1))

    masks = partner_table[:, 0]
    x_masks = jnp.bitwise_and(jnp.right_shift(masks, 1), 3)
    numbers = jnp.arange(rounds, dtype=jnp.int32)
    earlier = (x_masks[None, :] < x_masks[:, None]) | (
        (x_masks[None, :] == x_masks[:, None]) & (numbers[None, :] < numbers[:, None])
    )
    rank = jnp.sum(earlier.astype(jnp.int32), axis=1)
    ordered = jnp.sum(jnp.where(rank[None, :] == numbers[:, None], masks[None, :], 0), axis=1)
    table = np.zeros((rounds + 1, rounds + 1, rounds + 1), np.int32)
    for index, counts in enumerate(splits(rounds)):
        table[counts] = index
    counts = [jnp.sum((x_masks == mask).astype(jnp.int32)) for mask in (1, 2, 3)]
    branch = jnp.asarray(table)[counts[0], counts[1], counts[2]]
    cores = jnp.bitwise_and(ordered, 1)
    offsets = jnp.bitwise_and(jnp.bitwise_xor(my_z, jnp.right_shift(ordered, 3)) - my_z, 3)

    branches = [functools.partial(move_along_x, counts, rounds) for counts in splits(rounds)]

    def own_tile(shares, block, same):
        signs = jnp.where(same, 1.0, -1.0).astype(jnp.float32)
        logits = scale * dot_last(shares, block) + shift
        weights = (-scale * signs * jax.nn.sigmoid(-signs * logits)).astype(jnp.bfloat16)
        return dot(weights, block)

    first = myself * rows
    my_matches = lax.dynamic_slice_in_dim(matched_text_indices, begin, share, 0)
    photo_own = own_tile(
        pictures, sentence_vectors, my_matches[:, None] == first + lax.iota(jnp.int32, rows)[None, :]
    )
    wording_own = own_tile(
        texts,
        picture_vectors,
        matched_text_indices[None, :] == (first + begin + lax.iota(jnp.int32, share))[:, None],
    )

    def pick(versions):
        offset = offsets[:, None, None]
        return jnp.where(
            offset == 0,
            versions[0][None],
            jnp.where(
                offset == 1, versions[1][None], jnp.where(offset == 2, versions[2][None], versions[3][None])
            ),
        )

    stack = jnp.stack(
        [
            pick([pictures, above_pictures, across_pictures, below_pictures]),
            pick([texts, above_texts, across_texts, below_texts]),
        ],
        axis=1,
    )
    stack = lax.switch(branch, branches, stack)

    use_other = jnp.broadcast_to(cores[:, None], (rounds, share)).reshape(rounds * share, 1) == 1

    def cross_tiles(shares, block, other):
        products = jnp.where(use_other, dot_last(shares, other), dot_last(shares, block))
        weights = (scale * jax.nn.sigmoid(scale * products + shift)).astype(jnp.bfloat16)
        nothing = jnp.zeros_like(weights)
        return dot(jnp.where(use_other, nothing, weights), block) + dot(
            jnp.where(use_other, weights, nothing), other
        )

    photo = cross_tiles(stack[:, 0].reshape(rounds * share, span), sentence_vectors, other_texts)
    wording = cross_tiles(stack[:, 1].reshape(rounds * share, span), picture_vectors, other_pictures)
    back = jnp.stack(
        [photo.reshape(rounds, share, span), wording.reshape(rounds, share, span)], axis=1
    ).astype(jnp.float16)
    back = lax.switch(branch, branches, back)

    def of_offset(kind, offset):
        chosen = (offsets == offset)[:, None, None]
        return jnp.sum(jnp.where(chosen, back[:, kind].astype(jnp.float32), 0.0), axis=0)

    half = jnp.float16
    relayed_photo = permute(of_offset(0, 2).astype(half), z_pairs(1))
    relayed_wording = permute(of_offset(1, 2).astype(half), z_pairs(-1))
    up_wording = permute(of_offset(1, 1).astype(half), z_pairs(1))
    down_photo = permute(of_offset(0, 3).astype(half), z_pairs(-1))
    up_photo = permute((of_offset(0, 1) + relayed_photo.astype(jnp.float32)).astype(half), z_pairs(1))
    down_wording = permute((of_offset(1, 3) + relayed_wording.astype(jnp.float32)).astype(half), z_pairs(-1))
    photo_slopes = (
        photo_own + of_offset(0, 0) + down_photo.astype(jnp.float32) + up_photo.astype(jnp.float32)
    )
    wording_slopes = (
        wording_own + of_offset(1, 0) + up_wording.astype(jnp.float32) + down_wording.astype(jnp.float32)
    )
    return photo_slopes, wording_slopes


def solution(mesh):
    in_specs = (P("wide", None), P("wide", None), P("wide"), P(), P(), P())
    out_specs = (P(("wide", "narrow"), None), P(("wide", "narrow"), None))
    return jax.shard_map(local, mesh=mesh, in_specs=in_specs, out_specs=out_specs, check_vma=False)
```

```python
import functools
import jax
import jax.numpy as jnp
from jax import lax
from jax.experimental import pallas as pl
from jax.experimental.pallas import tpu as pltpu
from jax.sharding import PartitionSpec as P

WIDE = 32
Z_SETS = [[low + 8 * z for z in range(4)] for low in range(8)]
VMEM_LIMIT = 48 * 1024 * 1024


def xor_pairs(mask):
    return [(i, i ^ mask) for i in range(WIDE)]


def splits(rounds):
    return [
        (first, second, third)
        for first in range(rounds + 1)
        for second in range(rounds + 1 - first)
        for third in range(rounds + 1 - first - second)
    ]


def move_along_x(counts, rounds, stack):
    tall = stack.shape[0] // rounds
    start = rounds - sum(counts)
    pieces = [stack[: start * tall]] if start else []
    spans = {}
    for mask, count in enumerate(counts, 1):
        spans[mask] = (start, count)
        start += count
    moved = {}
    for mask in (2, 1, 3):
        begin, count = spans[mask]
        if count:
            piece = stack[begin * tall : (begin + count) * tall]
            moved[mask] = lax.ppermute(piece, "wide", xor_pairs(2 * mask))
    pieces += [moved[mask] for mask in sorted(moved)]
    return jnp.concatenate(pieces, axis=0) if len(pieces) > 1 else pieces[0]


def pick_kernel(rounds, table, gathered, stack, info):
    my_z = lax.axis_index("wide") // 8
    masks = [table[r, 0] for r in range(rounds)]
    x_masks = [(mask >> 1) & 3 for mask in masks]
    counts = [sum((x == k).astype(jnp.int32) for x in x_masks) for k in (1, 2, 3)]
    index = jnp.int32(0)
    for first in range(rounds):
        left = rounds - first
        index += jnp.where(counts[0] > first, (left + 1) * (left + 2) // 2, 0)
    left = rounds - counts[0]
    for second in range(rounds):
        index += jnp.where(counts[1] > second, left - second + 1, 0)
    info[0] = index + counts[2]
    tall = gathered.shape[1]
    for place in range(rounds):
        mask = jnp.int32(0)
        for r in range(rounds):
            rank = jnp.int32(0)
            for s in range(rounds):
                if s != r:
                    ahead = x_masks[s] <= x_masks[r] if s < r else x_masks[s] < x_masks[r]
                    rank += ahead.astype(jnp.int32)
            mask += jnp.where(rank == place, masks[r], 0)
        home = my_z ^ ((mask >> 3) & 3)
        info[1 + place] = mask & 1
        info[1 + rounds + place] = home
        stack[place * tall : (place + 1) * tall, :] = gathered[home]


def dot_last(left, right):
    return lax.dot_general(left, right, (((1,), (1,)), ((), ())), preferred_element_type=jnp.float32)


def dot(left, right):
    return jnp.dot(left, right, preferred_element_type=jnp.float32)


def grad_kernel(
    rounds, info, steepness, shift, matched, stack, pictures, texts, other_pictures, other_texts, back, own
):
    rows, span = pictures.shape
    share = stack.shape[0] // rounds // 2
    first = lax.axis_index("wide") * rows
    begin = pl.multiple_of(lax.axis_index("narrow") * share, share)
    scale = steepness[0] / span
    bias = shift[0]
    lanes = lax.broadcasted_iota(jnp.int32, (share, rows), 1)
    mine = begin + lax.broadcasted_iota(jnp.int32, (share, rows), 0)
    matches = jnp.broadcast_to(matched[...], (share, rows))
    my_match = jnp.sum(jnp.where(lanes == mine, matches, 0), axis=1, keepdims=True)
    for kind, (shares, block, other) in enumerate(
        [(pictures, texts, other_texts), (texts, pictures, other_pictures)]
    ):
        cross = [
            stack[(2 * place + kind) * share : (2 * place + kind + 1) * share, :] for place in range(rounds)
        ]
        left = jnp.concatenate([shares[pl.ds(begin, share), :]] + cross, axis=0)
        near = dot_last(left, block[...])
        far = dot_last(left[share:], other[...])
        same = (my_match == first + lanes) if kind == 0 else (matches == first + mine)
        signs = jnp.where(same, 1.0, -1.0).astype(jnp.float32)
        logits = scale * near[:share] + bias
        near_weights = [(-scale * signs * jax.nn.sigmoid(-signs * logits)).astype(jnp.bfloat16)]
        far_weights = []
        for place in range(rounds):
            apart = info[1 + place] == 1
            products = jnp.where(
                apart,
                far[place * share : (place + 1) * share],
                near[(place + 1) * share : (place + 2) * share],
            )
            weights = scale * jax.nn.sigmoid(scale * products + bias)
            near_weights.append(jnp.where(apart, 0.0, weights).astype(jnp.bfloat16))
            far_weights.append(jnp.where(apart, weights, 0.0).astype(jnp.bfloat16))
        near_slopes = dot(jnp.concatenate(near_weights, axis=0), block[...])
        far_slopes = dot(jnp.concatenate(far_weights, axis=0), other[...])
        own[kind * share : (kind + 1) * share, :] = near_slopes[:share]
        for place in range(rounds):
            back[(2 * place + kind) * share : (2 * place + kind + 1) * share, :] = (
                near_slopes[(place + 1) * share : (place + 2) * share]
                + far_slopes[place * share : (place + 1) * share]
            )


def local(
    picture_vectors,
    sentence_vectors,
    matched_text_indices,
    partner_table,
    trained_steepness,
    learned_shift,
):
    rows, span = picture_vectors.shape
    rounds = partner_table.shape[0]
    share = rows // lax.axis_size("narrow")
    begin = lax.axis_index("narrow") * share
    smem = pl.BlockSpec(memory_space=pltpu.SMEM)
    vmem = pl.BlockSpec(memory_space=pltpu.VMEM)

    other_pictures = lax.ppermute(picture_vectors, "wide", xor_pairs(1))
    other_texts = lax.ppermute(sentence_vectors, "wide", xor_pairs(1))
    shares = jnp.concatenate(
        [
            lax.dynamic_slice_in_dim(picture_vectors, begin, share, 0),
            lax.dynamic_slice_in_dim(sentence_vectors, begin, share, 0),
        ],
        axis=0,
    )
    gathered = lax.all_gather(shares, "wide", axis_index_groups=Z_SETS)
    stack, info = pl.pallas_call(
        functools.partial(pick_kernel, rounds),
        out_shape=[
            jax.ShapeDtypeStruct((rounds * 2 * share, span), jnp.bfloat16),
            jax.ShapeDtypeStruct((1 + 2 * rounds,), jnp.int32),
        ],
        in_specs=[smem, vmem],
        out_specs=[vmem, smem],
    )(partner_table, gathered)

    branches = [functools.partial(move_along_x, counts, rounds) for counts in splits(rounds)]
    stack = lax.switch(info[0], branches, stack)
    back, own = pl.pallas_call(
        functools.partial(grad_kernel, rounds),
        out_shape=[
            jax.ShapeDtypeStruct((rounds * 2 * share, span), jnp.float32),
            jax.ShapeDtypeStruct((2 * share, span), jnp.float32),
        ],
        in_specs=[smem, smem, smem] + [vmem] * 6,
        out_specs=[vmem, vmem],
        compiler_params=pltpu.CompilerParams(vmem_limit_bytes=VMEM_LIMIT),
    )(
        info,
        trained_steepness,
        learned_shift,
        matched_text_indices[None, :],
        stack,
        picture_vectors,
        sentence_vectors,
        other_pictures,
        other_texts,
    )
    back = lax.switch(info[0], branches, back.astype(jnp.float16))

    back = back.reshape(rounds, 2 * share, span).astype(jnp.float32)
    homes = info[1 + rounds :]
    sums = jnp.stack(
        [
            jnp.sum(jnp.where((homes == z)[:, None, None], back, 0.0), axis=0).astype(jnp.float16)
            for z in range(4)
        ],
        axis=0,
    )
    arrived = lax.all_to_all(sums, "wide", 0, 0, axis_index_groups=Z_SETS)
    slopes = own + jnp.sum(arrived.astype(jnp.float32), axis=0)
    return slopes[:share], slopes[share:]


def solution(mesh):
    in_specs = (P("wide", None), P("wide", None), P("wide"), P(), P(), P())
    out_specs = (P(("wide", "narrow"), None), P(("wide", "narrow"), None))
    return jax.shard_map(local, mesh=mesh, in_specs=in_specs, out_specs=out_specs, check_vma=False)
```

```python
import functools
import jax
import jax.numpy as jnp
from jax import lax
from jax.experimental import pallas as pl
from jax.experimental.pallas import tpu as pltpu
from jax.sharding import PartitionSpec as P

WIDE = 32
Z_SETS = [[low + 8 * z for z in range(4)] for low in range(8)]
VMEM_LIMIT = 48 * 1024 * 1024


def xor_pairs(mask):
    return [(i, i ^ mask) for i in range(WIDE)]


CAP = 2


def splits(rounds):
    sizes = range(CAP + 1)
    return [(a, b, c) for a in sizes for b in sizes for c in sizes if a + b + c <= rounds]


def move_along_x(counts, rounds, stack):
    tall = stack.shape[0] // rounds
    start = rounds - sum(counts)
    pieces = [stack[: start * tall]] if start else []
    spans = {}
    for mask, count in enumerate(counts, 1):
        spans[mask] = (start, count)
        start += count
    moved = {}
    for mask in (2, 1, 3):
        begin, count = spans[mask]
        if count:
            piece = stack[begin * tall : (begin + count) * tall]
            moved[mask] = lax.ppermute(piece, "wide", xor_pairs(2 * mask))
    pieces += [moved[mask] for mask in sorted(moved)]
    return jnp.concatenate(pieces, axis=0) if len(pieces) > 1 else pieces[0]


def move_spare(mask, count, rounds, stack):
    cut = stack.shape[0] // rounds * count
    moved = lax.ppermute(stack[:cut], "wide", xor_pairs(2 * mask))
    return jnp.concatenate([moved, stack[cut:]], axis=0) if count < rounds else moved


def exchange_x(rounds, main, spare, stack):
    stack = lax.switch(main, [functools.partial(move_along_x, c, rounds) for c in splits(rounds)], stack)
    moves = [lambda x: x]
    for mask in (1, 2, 3):
        for count in range(1, rounds - CAP + 1):
            moves.append(functools.partial(move_spare, mask, count, rounds))
    return lax.switch(spare, moves, stack)


def pick_kernel(rounds, table, *refs):
    shares, (stack, info) = refs[:4], refs[4:]
    my_z = lax.axis_index("wide") // 8
    masks = [table[r, 0] for r in range(rounds)]
    x_masks = [(mask >> 1) & 3 for mask in masks]
    keys = []
    for r in range(rounds):
        before = sum([(x_masks[s] == x_masks[r]).astype(jnp.int32) for s in range(r)], jnp.int32(0))
        spare = (x_masks[r] > 0) & (before >= CAP)
        keys.append(jnp.where(spare, 0, 1 + x_masks[r]))
    counts = [sum((x == k).astype(jnp.int32) for x in x_masks) for k in (1, 2, 3)]
    kept = [jnp.minimum(count, CAP) for count in counts]
    main = jnp.int32(0)
    for index, pattern in enumerate(splits(rounds)):
        hit = (kept[0] == pattern[0]) & (kept[1] == pattern[1]) & (kept[2] == pattern[2])
        main += jnp.where(hit, index, 0)
    spare = jnp.int32(0)
    for k in range(3):
        over = counts[k] - kept[k]
        spare += jnp.where(over > 0, k * (rounds - CAP) + over, 0)
    info[0] = main
    info[1] = spare
    tall = shares[0].shape[0]
    for place in range(rounds):
        mask = jnp.int32(0)
        for r in range(rounds):
            rank = jnp.int32(0)
            for s in range(rounds):
                if s != r:
                    ahead = keys[s] <= keys[r] if s < r else keys[s] < keys[r]
                    rank += ahead.astype(jnp.int32)
            mask += jnp.where(rank == place, masks[r], 0)
        z_mask = (mask >> 3) & 3
        info[2 + place] = mask & 1
        info[2 + rounds + place] = my_z ^ z_mask
        for z in range(4):

            @pl.when(z_mask == z)
            def _():
                stack[place * tall : (place + 1) * tall, :] = shares[z][...]


def dot_last(left, right):
    return lax.dot_general(left, right, (((1,), (1,)), ((), ())), preferred_element_type=jnp.float32)


def dot(left, right):
    return jnp.dot(left, right, preferred_element_type=jnp.float32)


def own_kernel(steepness, shift, matched, shares, pictures, texts, own):
    rows, span = pictures.shape
    share = own.shape[0] // 2
    first = lax.axis_index("wide") * rows
    begin = lax.axis_index("narrow") * share
    scale = steepness[0] / span
    bias = shift[0]
    lanes = lax.broadcasted_iota(jnp.int32, (share, rows), 1)
    mine = begin + lax.broadcasted_iota(jnp.int32, (share, rows), 0)
    matches = jnp.broadcast_to(matched[...], (share, rows))
    my_match = jnp.sum(jnp.where(lanes == mine, matches, 0), axis=1, keepdims=True)
    for kind, block in enumerate([texts, pictures]):
        span_rows = slice(kind * share, (kind + 1) * share)
        same = (my_match == first + lanes) if kind == 0 else (matches == first + mine)
        signs = jnp.where(same, 1.0, -1.0).astype(jnp.float32)
        logits = scale * dot_last(shares[span_rows, :], block[...]) + bias
        weights = (-scale * signs * jax.nn.sigmoid(-signs * logits)).astype(jnp.bfloat16)
        own[span_rows, :] = dot(weights, block[...])


def grad_kernel(rounds, info, steepness, shift, stack, pictures, texts, other_pictures, other_texts, back):
    span = pictures.shape[1]
    share = stack.shape[0] // rounds // 2
    scale = steepness[0] / span
    bias = shift[0]
    for kind, (block, other) in enumerate([(texts, other_texts), (pictures, other_pictures)]):
        left = jnp.concatenate(
            [stack[(2 * place + kind) * share : (2 * place + kind + 1) * share, :] for place in range(rounds)],
            axis=0,
        )
        near = dot_last(left, block[...])
        far = dot_last(left, other[...])
        near_weights = []
        far_weights = []
        for place in range(rounds):
            apart = info[2 + place] == 1
            span_rows = slice(place * share, (place + 1) * share)
            products = jnp.where(apart, far[span_rows], near[span_rows])
            weights = scale * jax.nn.sigmoid(scale * products + bias)
            near_weights.append(jnp.where(apart, 0.0, weights).astype(jnp.bfloat16))
            far_weights.append(jnp.where(apart, weights, 0.0).astype(jnp.bfloat16))
        slopes = dot(jnp.concatenate(near_weights, axis=0), block[...]) + dot(
            jnp.concatenate(far_weights, axis=0), other[...]
        )
        for place in range(rounds):
            back[(2 * place + kind) * share : (2 * place + kind + 1) * share, :] = slopes[
                place * share : (place + 1) * share
            ]


def local(
    picture_vectors,
    sentence_vectors,
    matched_text_indices,
    partner_table,
    trained_steepness,
    learned_shift,
):
    rows, span = picture_vectors.shape
    rounds = partner_table.shape[0]
    share = rows // lax.axis_size("narrow")
    begin = lax.axis_index("narrow") * share
    smem = pl.BlockSpec(memory_space=pltpu.SMEM)
    vmem = pl.BlockSpec(memory_space=pltpu.VMEM)

    other_pictures = lax.ppermute(picture_vectors, "wide", xor_pairs(1))
    other_texts = lax.ppermute(sentence_vectors, "wide", xor_pairs(1))
    shares = jnp.concatenate(
        [
            lax.dynamic_slice_in_dim(picture_vectors, begin, share, 0),
            lax.dynamic_slice_in_dim(sentence_vectors, begin, share, 0),
        ],
        axis=0,
    )
    by_z = [shares] + [lax.ppermute(shares, "wide", xor_pairs(8 * mask)) for mask in (1, 2, 3)]
    own = pl.pallas_call(
        own_kernel,
        out_shape=jax.ShapeDtypeStruct((2 * share, span), jnp.float32),
        in_specs=[smem, smem, vmem, vmem, vmem, vmem],
        out_specs=vmem,
        compiler_params=pltpu.CompilerParams(vmem_limit_bytes=VMEM_LIMIT),
    )(
        trained_steepness,
        learned_shift,
        matched_text_indices[None, :],
        shares,
        picture_vectors,
        sentence_vectors,
    )
    stack, info = pl.pallas_call(
        functools.partial(pick_kernel, rounds),
        out_shape=[
            jax.ShapeDtypeStruct((rounds * 2 * share, span), jnp.bfloat16),
            jax.ShapeDtypeStruct((2 + 2 * rounds,), jnp.int32),
        ],
        in_specs=[smem] + [vmem] * 4,
        out_specs=[vmem, smem],
    )(partner_table, *by_z)
    stack = exchange_x(rounds, info[0], info[1], stack)
    back = pl.pallas_call(
        functools.partial(grad_kernel, rounds),
        out_shape=jax.ShapeDtypeStruct((rounds * 2 * share, span), jnp.float32),
        in_specs=[smem, smem, smem] + [vmem] * 5,
        out_specs=vmem,
        compiler_params=pltpu.CompilerParams(vmem_limit_bytes=VMEM_LIMIT),
    )(
        info,
        trained_steepness,
        learned_shift,
        stack,
        picture_vectors,
        sentence_vectors,
        other_pictures,
        other_texts,
    )
    back = exchange_x(rounds, info[0], info[1], back.astype(jnp.float16))

    back = back.reshape(rounds, 2 * share, span).astype(jnp.float32)
    homes = info[2 + rounds :]
    sums = jnp.stack(
        [
            jnp.sum(jnp.where((homes == z)[:, None, None], back, 0.0), axis=0).astype(jnp.float16)
            for z in range(4)
        ],
        axis=0,
    )
    arrived = lax.all_to_all(sums, "wide", 0, 0, axis_index_groups=Z_SETS)
    slopes = own + jnp.sum(arrived.astype(jnp.float32), axis=0)
    return slopes[:share], slopes[share:]


def solution(mesh):
    in_specs = (P("wide", None), P("wide", None), P("wide"), P(), P(), P())
    out_specs = (P(("wide", "narrow"), None), P(("wide", "narrow"), None))
    return jax.shard_map(local, mesh=mesh, in_specs=in_specs, out_specs=out_specs, check_vma=False)
```

```python
import functools
import jax
import jax.numpy as jnp
from jax import lax
from jax.experimental import pallas as pl
from jax.experimental.pallas import tpu as pltpu
from jax.sharding import PartitionSpec as P

WIDE = 32
Z_SETS = [[low + 8 * z for z in range(4)] for low in range(8)]
PICK_VMEM = 4 * 1024 * 1024
OWN_VMEM = 12 * 1024 * 1024
GRAD_VMEM = 24 * 1024 * 1024


def xor_pairs(mask):
    return [(i, i ^ mask) for i in range(WIDE)]


CAP = 2


def splits(rounds):
    sizes = range(CAP + 1)
    return [(a, b, c) for a in sizes for b in sizes for c in sizes if a + b + c <= rounds]


def move_along_x(counts, rounds, stack):
    tall = stack.shape[0] // rounds
    start = rounds - sum(counts)
    pieces = [stack[: start * tall]] if start else []
    spans = {}
    for mask, count in enumerate(counts, 1):
        spans[mask] = (start, count)
        start += count
    moved = {}
    for mask in (2, 1, 3):
        begin, count = spans[mask]
        if count:
            piece = stack[begin * tall : (begin + count) * tall]
            moved[mask] = lax.ppermute(piece, "wide", xor_pairs(2 * mask))
    pieces += [moved[mask] for mask in sorted(moved)]
    return jnp.concatenate(pieces, axis=0) if len(pieces) > 1 else pieces[0]


def move_spare(mask, count, rounds, stack):
    cut = stack.shape[0] // rounds * count
    moved = lax.ppermute(stack[:cut], "wide", xor_pairs(2 * mask))
    return jnp.concatenate([moved, stack[cut:]], axis=0) if count < rounds else moved


def exchange_x(rounds, main, spare, stack):
    stack = lax.switch(main, [functools.partial(move_along_x, c, rounds) for c in splits(rounds)], stack)
    moves = [lambda x: x]
    for mask in (1, 2, 3):
        for count in range(1, rounds - CAP + 1):
            moves.append(functools.partial(move_spare, mask, count, rounds))
    return lax.switch(spare, moves, stack)


def order_kernel(rounds, table, main, spare, info):
    my_z = lax.axis_index("wide") // 8
    masks = [table[r, 0] for r in range(rounds)]
    x_masks = [(mask >> 1) & 3 for mask in masks]
    keys = []
    for r in range(rounds):
        before = sum([(x_masks[s] == x_masks[r]).astype(jnp.int32) for s in range(r)], jnp.int32(0))
        beyond = (x_masks[r] > 0) & (before >= CAP)
        keys.append(jnp.where(beyond, 0, 1 + x_masks[r]))
    counts = [sum((x == k).astype(jnp.int32) for x in x_masks) for k in (1, 2, 3)]
    kept = [jnp.minimum(count, CAP) for count in counts]
    index = jnp.int32(0)
    for place, pattern in enumerate(splits(rounds)):
        hit = (kept[0] == pattern[0]) & (kept[1] == pattern[1]) & (kept[2] == pattern[2])
        index += jnp.where(hit, place, 0)
    main[0] = index
    index = jnp.int32(0)
    for k in range(3):
        over = counts[k] - kept[k]
        index += jnp.where(over > 0, k * (rounds - CAP) + over, 0)
    spare[0] = index
    for place in range(rounds):
        mask = jnp.int32(0)
        for r in range(rounds):
            rank = jnp.int32(0)
            for s in range(rounds):
                if s != r:
                    ahead = keys[s] <= keys[r] if s < r else keys[s] < keys[r]
                    rank += ahead.astype(jnp.int32)
            mask += jnp.where(rank == place, masks[r], 0)
        info[place] = mask & 1
        info[rounds + place] = (mask >> 3) & 3
        info[2 * rounds + place] = my_z ^ ((mask >> 3) & 3)


def pick_kernel(rounds, info, *refs):
    shares, stack = refs[:4], refs[4]
    tall = shares[0].shape[0]
    for place in range(rounds):
        z_mask = info[rounds + place]
        for z in range(4):

            @pl.when(z_mask == z)
            def _():
                stack[place * tall : (place + 1) * tall, :] = shares[z][...]


def dot_last(left, right):
    return lax.dot_general(left, right, (((1,), (1,)), ((), ())), preferred_element_type=jnp.float32)


def dot(left, right):
    return jnp.dot(left, right, preferred_element_type=jnp.float32)


def own_kernel(steepness, shift, matched, shares, pictures, texts, own):
    rows, span = pictures.shape
    share = own.shape[0] // 2
    first = lax.axis_index("wide") * rows
    begin = lax.axis_index("narrow") * share
    scale = steepness[0] / span
    bias = shift[0]
    lanes = lax.broadcasted_iota(jnp.int32, (share, rows), 1)
    mine = begin + lax.broadcasted_iota(jnp.int32, (share, rows), 0)
    matches = jnp.broadcast_to(matched[...], (share, rows))
    my_match = jnp.sum(jnp.where(lanes == mine, matches, 0), axis=1, keepdims=True)
    for kind, block in enumerate([texts, pictures]):
        span_rows = slice(kind * share, (kind + 1) * share)
        same = (my_match == first + lanes) if kind == 0 else (matches == first + mine)
        signs = jnp.where(same, 1.0, -1.0).astype(jnp.float32)
        logits = scale * dot_last(shares[span_rows, :], block[...]) + bias
        weights = (-scale * signs * jax.nn.sigmoid(-signs * logits)).astype(jnp.bfloat16)
        own[span_rows, :] = dot(weights, block[...])


def grad_kernel(rounds, info, steepness, shift, stack, pictures, texts, other_pictures, other_texts, back):
    span = pictures.shape[1]
    share = stack.shape[0] // rounds // 2
    scale = steepness[0] / span
    bias = shift[0]
    for kind, (block, other) in enumerate([(texts, other_texts), (pictures, other_pictures)]):
        left = jnp.concatenate(
            [stack[(2 * place + kind) * share : (2 * place + kind + 1) * share, :] for place in range(rounds)],
            axis=0,
        )
        near = dot_last(left, block[...])
        far = dot_last(left, other[...])
        near_weights = []
        far_weights = []
        for place in range(rounds):
            apart = info[place] == 1
            span_rows = slice(place * share, (place + 1) * share)
            products = jnp.where(apart, far[span_rows], near[span_rows])
            weights = scale * jax.nn.sigmoid(scale * products + bias)
            near_weights.append(jnp.where(apart, 0.0, weights).astype(jnp.bfloat16))
            far_weights.append(jnp.where(apart, weights, 0.0).astype(jnp.bfloat16))
        slopes = dot(jnp.concatenate(near_weights, axis=0), block[...]) + dot(
            jnp.concatenate(far_weights, axis=0), other[...]
        )
        for place in range(rounds):
            back[(2 * place + kind) * share : (2 * place + kind + 1) * share, :] = slopes[
                place * share : (place + 1) * share
            ]


def local(
    picture_vectors,
    sentence_vectors,
    matched_text_indices,
    partner_table,
    trained_steepness,
    learned_shift,
):
    rows, span = picture_vectors.shape
    rounds = partner_table.shape[0]
    share = rows // lax.axis_size("narrow")
    begin = lax.axis_index("narrow") * share
    smem = pl.BlockSpec(memory_space=pltpu.SMEM)
    vmem = pl.BlockSpec(memory_space=pltpu.VMEM)

    other_pictures = lax.ppermute(picture_vectors, "wide", xor_pairs(1))
    other_texts = lax.ppermute(sentence_vectors, "wide", xor_pairs(1))
    shares = jnp.concatenate(
        [
            lax.dynamic_slice_in_dim(picture_vectors, begin, share, 0),
            lax.dynamic_slice_in_dim(sentence_vectors, begin, share, 0),
        ],
        axis=0,
    )
    by_z = [shares] + [lax.ppermute(shares, "wide", xor_pairs(8 * mask)) for mask in (1, 2, 3)]
    own = pl.pallas_call(
        own_kernel,
        out_shape=jax.ShapeDtypeStruct((2 * share, span), jnp.float32),
        in_specs=[smem, smem, vmem, vmem, vmem, vmem],
        out_specs=vmem,
        compiler_params=pltpu.CompilerParams(vmem_limit_bytes=OWN_VMEM),
    )(
        trained_steepness,
        learned_shift,
        matched_text_indices[None, :],
        shares,
        picture_vectors,
        sentence_vectors,
    )
    main, spare, info = pl.pallas_call(
        functools.partial(order_kernel, rounds),
        out_shape=[
            jax.ShapeDtypeStruct((1,), jnp.int32),
            jax.ShapeDtypeStruct((1,), jnp.int32),
            jax.ShapeDtypeStruct((3 * rounds,), jnp.int32),
        ],
        in_specs=[smem],
        out_specs=[smem, smem, smem],
    )(partner_table)
    stack = pl.pallas_call(
        functools.partial(pick_kernel, rounds),
        out_shape=jax.ShapeDtypeStruct((rounds * 2 * share, span), jnp.bfloat16),
        in_specs=[smem] + [vmem] * 4,
        out_specs=vmem,
        compiler_params=pltpu.CompilerParams(vmem_limit_bytes=PICK_VMEM),
    )(info, *by_z)
    stack = exchange_x(rounds, main[0], spare[0], stack)
    back = pl.pallas_call(
        functools.partial(grad_kernel, rounds),
        out_shape=jax.ShapeDtypeStruct((rounds * 2 * share, span), jnp.float32),
        in_specs=[smem, smem, smem] + [vmem] * 5,
        out_specs=vmem,
        compiler_params=pltpu.CompilerParams(vmem_limit_bytes=GRAD_VMEM),
    )(
        info,
        trained_steepness,
        learned_shift,
        stack,
        picture_vectors,
        sentence_vectors,
        other_pictures,
        other_texts,
    )
    back = exchange_x(rounds, main[0], spare[0], back.astype(jnp.float16))

    back = back.reshape(rounds, 2 * share, span).astype(jnp.float32)
    homes = info[2 * rounds :]
    sums = jnp.stack(
        [
            jnp.sum(jnp.where((homes == z)[:, None, None], back, 0.0), axis=0).astype(jnp.float16)
            for z in range(4)
        ],
        axis=0,
    )
    arrived = lax.all_to_all(sums, "wide", 0, 0, axis_index_groups=Z_SETS)
    arrived = arrived.astype(jnp.float32)
    photo_slopes = own[:share] + jnp.sum(arrived[:, :share], axis=0)
    wording_slopes = own[share:] + jnp.sum(arrived[:, share:], axis=0)
    return photo_slopes, wording_slopes


def solution(mesh):
    in_specs = (P("wide", None), P("wide", None), P("wide"), P(), P(), P())
    out_specs = (P(("wide", "narrow"), None), P(("wide", "narrow"), None))
    return jax.shard_map(local, mesh=mesh, in_specs=in_specs, out_specs=out_specs, check_vma=False)
```

```python
import functools
import jax
import jax.numpy as jnp
from jax import lax
from jax.experimental import pallas as pl
from jax.experimental.pallas import tpu as pltpu
from jax.sharding import PartitionSpec as P

WIDE = 32
Z_SETS = [[low + 8 * z for z in range(4)] for low in range(8)]
X_SETS = [[8 * z + 2 * x + core for x in range(4)] for z in range(4) for core in range(2)]
CAP = 2
MAIN = 4 * CAP
PICK_VMEM = 8 * 1024 * 1024
OWN_VMEM = 12 * 1024 * 1024
GRAD_VMEM = 24 * 1024 * 1024


def xor_pairs(mask):
    return [(i, i ^ mask) for i in range(WIDE)]


def move_spare(mask, count, stack):
    moved = lax.ppermute(stack[:count], "wide", xor_pairs(2 * mask))
    return jnp.concatenate([moved, stack[count:]], axis=0) if count < stack.shape[0] else moved


def exchange_x(spare, main, rest):
    places, tall, span = main.shape
    sent = main.reshape(4, CAP * tall, span)
    main = lax.all_to_all(sent, "wide", 0, 0, axis_index_groups=X_SETS).reshape(places, tall, span)
    moves = [lambda stack: stack]
    for mask in (1, 2, 3):
        for count in range(1, rest.shape[0] + 1):
            moves.append(functools.partial(move_spare, mask, count))
    return main, lax.switch(spare, moves, rest)


def order_kernel(rounds, table, spare, info, homes):
    my_z = lax.axis_index("wide") // 8
    my_x = (lax.axis_index("wide") // 2) % 4
    masks = [table[r, 0] & (WIDE - 1) for r in range(rounds)]
    x_masks = [(mask >> 1) & 3 for mask in masks]
    for place in range(MAIN + rounds - CAP):
        homes[place] = -1
    beyond = jnp.int32(0)
    index = jnp.int32(0)
    for r in range(rounds):
        before = sum([(x_masks[s] == x_masks[r]).astype(jnp.int32) for s in range(r)], jnp.int32(0))
        fits = before < CAP
        place = jnp.where(fits, (my_x ^ x_masks[r]) * CAP + before, MAIN + beyond)
        beyond += jnp.where(fits, 0, 1)
        over = before - CAP + 1
        index = jnp.where(fits | (x_masks[r] == 0), index, (x_masks[r] - 1) * (rounds - CAP) + over)
        info[r] = masks[r] & 1
        info[rounds + r] = masks[r] >> 3
        info[2 * rounds + r] = place
        homes[place] = my_z ^ (masks[r] >> 3)
    spare[0] = index


def pick_kernel(rounds, info, *refs):
    shares, (main, rest) = refs[:4], refs[4:]
    main[...] = jnp.zeros_like(main)
    rest[...] = jnp.zeros_like(rest)
    for r in range(rounds):
        z_mask = info[rounds + r]
        place = info[2 * rounds + r]
        for z in range(4):

            @pl.when((z_mask == z) & (place < MAIN))
            def _():
                main[place] = shares[z][...]

            @pl.when((z_mask == z) & (place >= MAIN))
            def _():
                rest[place - MAIN] = shares[z][...]


def dot_last(left, right):
    return lax.dot_general(left, right, (((1,), (1,)), ((), ())), preferred_element_type=jnp.float32)


def dot(left, right):
    return jnp.dot(left, right, preferred_element_type=jnp.float32)


def own_kernel(steepness, shift, matched, shares, pictures, texts, own):
    rows, span = pictures.shape
    share = own.shape[0] // 2
    first = lax.axis_index("wide") * rows
    begin = lax.axis_index("narrow") * share
    scale = steepness[0] / span
    bias = shift[0]
    lanes = lax.broadcasted_iota(jnp.int32, (share, rows), 1)
    mine = begin + lax.broadcasted_iota(jnp.int32, (share, rows), 0)
    matches = jnp.broadcast_to(matched[...], (share, rows))
    my_match = jnp.sum(jnp.where(lanes == mine, matches, 0), axis=1, keepdims=True)
    for kind, block in enumerate([texts, pictures]):
        span_rows = slice(kind * share, (kind + 1) * share)
        same = (my_match == first + lanes) if kind == 0 else (matches == first + mine)
        signs = jnp.where(same, 1.0, -1.0).astype(jnp.float32)
        logits = scale * dot_last(shares[span_rows, :], block[...]) + bias
        weights = (-scale * signs * jax.nn.sigmoid(-signs * logits)).astype(jnp.bfloat16)
        own[span_rows, :] = dot(weights, block[...])


def grad_kernel(
    rounds,
    info,
    steepness,
    shift,
    main,
    rest,
    pictures,
    texts,
    other_pictures,
    other_texts,
    back_main,
    back_rest,
    left,
):
    span = pictures.shape[1]
    share = main.shape[1] // 2
    scale = steepness[0] / span
    bias = shift[0]
    back_main[...] = jnp.zeros_like(back_main)
    back_rest[...] = jnp.zeros_like(back_rest)
    for r in range(rounds):
        place = info[2 * rounds + r]
        for kind in range(2):
            kind_rows = slice(kind * share, (kind + 1) * share)
            left_rows = slice(r * share, (r + 1) * share)

            @pl.when(place < MAIN)
            def _():
                left[kind, left_rows, :] = main[place, kind_rows, :]

            @pl.when(place >= MAIN)
            def _():
                left[kind, left_rows, :] = rest[place - MAIN, kind_rows, :]

    for kind, (block, other) in enumerate([(texts, other_texts), (pictures, other_pictures)]):
        kind_rows = slice(kind * share, (kind + 1) * share)
        near = dot_last(left[kind], block[...])
        far = dot_last(left[kind], other[...])
        near_weights = []
        far_weights = []
        for r in range(rounds):
            apart = info[r] == 1
            left_rows = slice(r * share, (r + 1) * share)
            products = jnp.where(apart, far[left_rows], near[left_rows])
            weights = scale * jax.nn.sigmoid(scale * products + bias)
            near_weights.append(jnp.where(apart, 0.0, weights).astype(jnp.bfloat16))
            far_weights.append(jnp.where(apart, weights, 0.0).astype(jnp.bfloat16))
        slopes = dot(jnp.concatenate(near_weights, axis=0), block[...]) + dot(
            jnp.concatenate(far_weights, axis=0), other[...]
        )
        for r in range(rounds):
            place = info[2 * rounds + r]
            slope = slopes[r * share : (r + 1) * share]

            @pl.when(place < MAIN)
            def _():
                back_main[place, kind_rows, :] = slope

            @pl.when(place >= MAIN)
            def _():
                back_rest[place - MAIN, kind_rows, :] = slope


def local(
    picture_vectors,
    sentence_vectors,
    matched_text_indices,
    partner_table,
    trained_steepness,
    learned_shift,
):
    rows, span = picture_vectors.shape
    rounds = partner_table.shape[0]
    share = rows // lax.axis_size("narrow")
    begin = lax.axis_index("narrow") * share
    smem = pl.BlockSpec(memory_space=pltpu.SMEM)
    vmem = pl.BlockSpec(memory_space=pltpu.VMEM)

    other_pictures = lax.ppermute(picture_vectors, "wide", xor_pairs(1))
    other_texts = lax.ppermute(sentence_vectors, "wide", xor_pairs(1))
    shares = jnp.concatenate(
        [
            lax.dynamic_slice_in_dim(picture_vectors, begin, share, 0),
            lax.dynamic_slice_in_dim(sentence_vectors, begin, share, 0),
        ],
        axis=0,
    )
    by_z = [shares] + [lax.ppermute(shares, "wide", xor_pairs(8 * mask)) for mask in (1, 2, 3)]
    own = pl.pallas_call(
        own_kernel,
        out_shape=jax.ShapeDtypeStruct((2 * share, span), jnp.float32),
        in_specs=[smem, smem, vmem, vmem, vmem, vmem],
        out_specs=vmem,
        compiler_params=pltpu.CompilerParams(vmem_limit_bytes=OWN_VMEM),
    )(
        trained_steepness,
        learned_shift,
        matched_text_indices[None, :],
        shares,
        picture_vectors,
        sentence_vectors,
    )
    spare, info, homes = pl.pallas_call(
        functools.partial(order_kernel, rounds),
        out_shape=[
            jax.ShapeDtypeStruct((1,), jnp.int32),
            jax.ShapeDtypeStruct((3 * rounds,), jnp.int32),
            jax.ShapeDtypeStruct((MAIN + rounds - CAP,), jnp.int32),
        ],
        in_specs=[smem],
        out_specs=[smem, smem, smem],
        compiler_params=pltpu.CompilerParams(vmem_limit_bytes=PICK_VMEM),
    )(partner_table)
    main_shape = (MAIN, 2 * share, span)
    rest_shape = (rounds - CAP, 2 * share, span)
    main, rest = pl.pallas_call(
        functools.partial(pick_kernel, rounds),
        out_shape=[
            jax.ShapeDtypeStruct(main_shape, jnp.bfloat16),
            jax.ShapeDtypeStruct(rest_shape, jnp.bfloat16),
        ],
        in_specs=[smem] + [vmem] * 4,
        out_specs=[vmem, vmem],
        compiler_params=pltpu.CompilerParams(vmem_limit_bytes=PICK_VMEM),
    )(info, *by_z)
    main, rest = exchange_x(spare[0], main, rest)
    main, rest = pl.pallas_call(
        functools.partial(grad_kernel, rounds),
        out_shape=[
            jax.ShapeDtypeStruct(main_shape, jnp.float32),
            jax.ShapeDtypeStruct(rest_shape, jnp.float32),
        ],
        in_specs=[smem, smem, smem] + [vmem] * 6,
        out_specs=[vmem, vmem],
        scratch_shapes=[pltpu.VMEM((2, rounds * share, span), jnp.bfloat16)],
        compiler_params=pltpu.CompilerParams(vmem_limit_bytes=GRAD_VMEM),
    )(
        info,
        trained_steepness,
        learned_shift,
        main,
        rest,
        picture_vectors,
        sentence_vectors,
        other_pictures,
        other_texts,
    )
    main, rest = exchange_x(spare[0], main.astype(jnp.float16), rest.astype(jnp.float16))

    def of_home(z):
        mine = (homes == z)[:, None, None]
        return (
            jnp.sum(jnp.where(mine[:MAIN], main.astype(jnp.float32), 0.0), axis=0)
            + jnp.sum(jnp.where(mine[MAIN:], rest.astype(jnp.float32), 0.0), axis=0)
        ).astype(jnp.float16)

    sums = jnp.stack([of_home(z) for z in range(4)], axis=0)
    arrived = lax.all_to_all(sums, "wide", 0, 0, axis_index_groups=Z_SETS)
    arrived = arrived.astype(jnp.float32)
    photo_slopes = own[:share] + jnp.sum(arrived[:, :share], axis=0)
    wording_slopes = own[share:] + jnp.sum(arrived[:, share:], axis=0)
    return photo_slopes, wording_slopes


def solution(mesh):
    in_specs = (P("wide", None), P("wide", None), P("wide"), P(), P(), P())
    out_specs = (P(("wide", "narrow"), None), P(("wide", "narrow"), None))
    return jax.shard_map(local, mesh=mesh, in_specs=in_specs, out_specs=out_specs, check_vma=False)
```

```python
import functools
import jax
import jax.numpy as jnp
from jax import lax
from jax.experimental import pallas as pl
from jax.experimental.pallas import tpu as pltpu
from jax.sharding import PartitionSpec as P

WIDE = 32
Z_SETS = [[low + 8 * z for z in range(4)] for low in range(8)]
X_SETS = [[8 * z + 2 * x + core for x in range(4)] for z in range(4) for core in range(2)]
CAP = 2
MAIN = 4 * CAP
PICK_VMEM = 8 * 1024 * 1024
GRAD_VMEM = 24 * 1024 * 1024


def xor_pairs(mask):
    return [(i, i ^ mask) for i in range(WIDE)]


def move_spare(mask, count, stack):
    moved = lax.ppermute(stack[:count], "wide", xor_pairs(2 * mask))
    return jnp.concatenate([moved, stack[count:]], axis=0) if count < stack.shape[0] else moved


def exchange_x(spare, main, rest):
    places, tall, span = main.shape
    moves = [lambda stack: stack]
    for mask in (1, 2, 3):
        for count in range(1, rest.shape[0] + 1):
            moves.append(functools.partial(move_spare, mask, count))
    main, rest = lax.optimization_barrier((main, lax.switch(spare, moves, rest)))
    sent = main.reshape(4, CAP * tall, span)
    main = lax.all_to_all(sent, "wide", 0, 0, axis_index_groups=X_SETS).reshape(places, tall, span)
    return lax.optimization_barrier((main, rest))


def pick_kernel(rounds, table, gathered, main, rest, spare, info, homes):
    my_z = lax.axis_index("wide") // 8
    my_x = (lax.axis_index("wide") // 2) % 4
    masks = [table[r, 0] & (WIDE - 1) for r in range(rounds)]
    x_masks = [(mask >> 1) & 3 for mask in masks]
    for place in range(MAIN + rounds - CAP):
        homes[place] = -1
    main[...] = jnp.zeros_like(main)
    rest[...] = jnp.zeros_like(rest)
    beyond = jnp.int32(0)
    index = jnp.int32(0)
    for r in range(rounds):
        before = sum([(x_masks[s] == x_masks[r]).astype(jnp.int32) for s in range(r)], jnp.int32(0))
        fits = before < CAP
        place = jnp.where(fits, (my_x ^ x_masks[r]) * CAP + before, MAIN + beyond)
        beyond += jnp.where(fits, 0, 1)
        over = before - CAP + 1
        index = jnp.where(fits | (x_masks[r] == 0), index, (x_masks[r] - 1) * (rounds - CAP) + over)
        home = my_z ^ (masks[r] >> 3)
        info[r] = masks[r] & 1
        info[rounds + r] = place
        homes[place] = home

        @pl.when(place < MAIN)
        def _():
            main[place] = gathered[home]

        @pl.when(place >= MAIN)
        def _():
            rest[place - MAIN] = gathered[home]

    spare[0] = index


def dot_last(left, right):
    return lax.dot_general(left, right, (((1,), (1,)), ((), ())), preferred_element_type=jnp.float32)


def dot(left, right):
    return jnp.dot(left, right, preferred_element_type=jnp.float32)


def grad_kernel(
    rounds,
    info,
    steepness,
    shift,
    matched,
    shares,
    main,
    rest,
    pictures,
    texts,
    other_pictures,
    other_texts,
    back_main,
    back_rest,
    own,
    left,
):
    rows, span = pictures.shape
    share = main.shape[1] // 2
    first = lax.axis_index("wide") * rows
    begin = lax.axis_index("narrow") * share
    scale = steepness[0] / span
    bias = shift[0]
    lanes = lax.broadcasted_iota(jnp.int32, (share, rows), 1)
    mine = begin + lax.broadcasted_iota(jnp.int32, (share, rows), 0)
    matches = jnp.broadcast_to(matched[...], (share, rows))
    my_match = jnp.sum(jnp.where(lanes == mine, matches, 0), axis=1, keepdims=True)
    back_main[...] = jnp.zeros_like(back_main)
    back_rest[...] = jnp.zeros_like(back_rest)
    for kind in range(2):
        kind_rows = slice(kind * share, (kind + 1) * share)
        left[kind, rounds * share :, :] = shares[kind_rows, :]
        for r in range(rounds):
            place = info[rounds + r]
            left_rows = slice(r * share, (r + 1) * share)

            @pl.when(place < MAIN)
            def _():
                left[kind, left_rows, :] = main[place, kind_rows, :]

            @pl.when(place >= MAIN)
            def _():
                left[kind, left_rows, :] = rest[place - MAIN, kind_rows, :]

    for kind, (block, other) in enumerate([(texts, other_texts), (pictures, other_pictures)]):
        kind_rows = slice(kind * share, (kind + 1) * share)
        near = dot_last(left[kind], block[...])
        far = dot_last(left[kind, : rounds * share, :], other[...])
        near_weights = []
        far_weights = []
        for r in range(rounds):
            apart = info[r] == 1
            left_rows = slice(r * share, (r + 1) * share)
            products = jnp.where(apart, far[left_rows], near[left_rows])
            weights = scale * jax.nn.sigmoid(scale * products + bias)
            near_weights.append(jnp.where(apart, 0.0, weights).astype(jnp.bfloat16))
            far_weights.append(jnp.where(apart, weights, 0.0).astype(jnp.bfloat16))
        same = (my_match == first + lanes) if kind == 0 else (matches == first + mine)
        signs = jnp.where(same, 1.0, -1.0).astype(jnp.float32)
        logits = scale * near[rounds * share :] + bias
        near_weights.append((-scale * signs * jax.nn.sigmoid(-signs * logits)).astype(jnp.bfloat16))
        near_slopes = dot(jnp.concatenate(near_weights, axis=0), block[...])
        slopes = near_slopes[: rounds * share] + dot(jnp.concatenate(far_weights, axis=0), other[...])
        own[kind_rows, :] = near_slopes[rounds * share :]
        for r in range(rounds):
            place = info[rounds + r]
            slope = slopes[r * share : (r + 1) * share]

            @pl.when(place < MAIN)
            def _():
                back_main[place, kind_rows, :] = slope

            @pl.when(place >= MAIN)
            def _():
                back_rest[place - MAIN, kind_rows, :] = slope


def local(
    picture_vectors,
    sentence_vectors,
    matched_text_indices,
    partner_table,
    trained_steepness,
    learned_shift,
):
    rows, span = picture_vectors.shape
    rounds = partner_table.shape[0]
    share = rows // lax.axis_size("narrow")
    begin = lax.axis_index("narrow") * share
    smem = pl.BlockSpec(memory_space=pltpu.SMEM)
    vmem = pl.BlockSpec(memory_space=pltpu.VMEM)

    other_pictures = lax.ppermute(picture_vectors, "wide", xor_pairs(1))
    other_texts = lax.ppermute(sentence_vectors, "wide", xor_pairs(1))
    shares = jnp.concatenate(
        [
            lax.dynamic_slice_in_dim(picture_vectors, begin, share, 0),
            lax.dynamic_slice_in_dim(sentence_vectors, begin, share, 0),
        ],
        axis=0,
    )
    gathered = lax.all_gather(shares, "wide", axis_index_groups=Z_SETS)
    main_shape = (MAIN, 2 * share, span)
    rest_shape = (rounds - CAP, 2 * share, span)
    main, rest, spare, info, homes = pl.pallas_call(
        functools.partial(pick_kernel, rounds),
        out_shape=[
            jax.ShapeDtypeStruct(main_shape, jnp.bfloat16),
            jax.ShapeDtypeStruct(rest_shape, jnp.bfloat16),
            jax.ShapeDtypeStruct((1,), jnp.int32),
            jax.ShapeDtypeStruct((2 * rounds,), jnp.int32),
            jax.ShapeDtypeStruct((MAIN + rounds - CAP,), jnp.int32),
        ],
        in_specs=[smem, vmem],
        out_specs=[vmem, vmem, smem, smem, smem],
        compiler_params=pltpu.CompilerParams(vmem_limit_bytes=PICK_VMEM),
    )(partner_table, gathered)
    main, rest = exchange_x(spare[0], main, rest)
    main, rest, own = pl.pallas_call(
        functools.partial(grad_kernel, rounds),
        out_shape=[
            jax.ShapeDtypeStruct(main_shape, jnp.float32),
            jax.ShapeDtypeStruct(rest_shape, jnp.float32),
            jax.ShapeDtypeStruct((2 * share, span), jnp.float32),
        ],
        in_specs=[smem, smem, smem] + [vmem] * 8,
        out_specs=[vmem, vmem, vmem],
        scratch_shapes=[pltpu.VMEM((2, (rounds + 1) * share, span), jnp.bfloat16)],
        compiler_params=pltpu.CompilerParams(vmem_limit_bytes=GRAD_VMEM),
    )(
        info,
        trained_steepness,
        learned_shift,
        matched_text_indices[None, :],
        shares,
        main,
        rest,
        picture_vectors,
        sentence_vectors,
        other_pictures,
        other_texts,
    )
    main, rest = exchange_x(spare[0], main.astype(jnp.float16), rest.astype(jnp.float16))
    main, homes = lax.optimization_barrier((main, homes))

    def by_home(stack, places):
        chosen = places[None, :] == jnp.arange(4, dtype=jnp.int32)[:, None]
        return jnp.sum(jnp.where(chosen[:, :, None, None], stack[None].astype(jnp.float32), 0.0), axis=1)

    sums = (by_home(main, homes[:MAIN]) + by_home(rest, homes[MAIN:])).astype(jnp.float16)
    arrived = lax.all_to_all(sums, "wide", 0, 0, axis_index_groups=Z_SETS)
    arrived, own = lax.optimization_barrier((arrived, own))
    slopes = own + jnp.sum(arrived.astype(jnp.float32), axis=0)
    return slopes[:share], slopes[share:]


def solution(mesh):
    in_specs = (P("wide", None), P("wide", None), P("wide"), P(), P(), P())
    out_specs = (P(("wide", "narrow"), None), P(("wide", "narrow"), None))
    return jax.shard_map(local, mesh=mesh, in_specs=in_specs, out_specs=out_specs, check_vma=False)
```

```python
import functools
import jax
import jax.numpy as jnp
from jax import lax
from jax.experimental import pallas as pl
from jax.experimental.pallas import tpu as pltpu
from jax.sharding import PartitionSpec as P

WIDE = 32
Z_SETS = [[low + 8 * z for z in range(4)] for low in range(8)]
X_SETS = [[8 * z + 2 * x + core for x in range(4)] for z in range(4) for core in range(2)]
CAP = 2
MAIN = 4 * CAP
PICK_VMEM = 8 * 1024 * 1024
GRAD_VMEM = 24 * 1024 * 1024


def xor_pairs(mask):
    return [(i, i ^ mask) for i in range(WIDE)]


def move_spare(mask, count, stack):
    moved = lax.ppermute(stack[:count], "wide", xor_pairs(2 * mask))
    return jnp.concatenate([moved, stack[count:]], axis=0) if count < stack.shape[0] else moved


def exchange_x(spare, main, rest, alone):
    places, tall, span = main.shape
    moves = [lambda stack: stack]
    for mask in (1, 2, 3):
        for count in range(1, rest.shape[0] + 1):
            moves.append(functools.partial(move_spare, mask, count))
    rest = lax.switch(spare, moves, rest)
    if alone:
        main, rest = lax.optimization_barrier((main, rest))
    sent = main.reshape(4, CAP * tall, span)
    main = lax.all_to_all(sent, "wide", 0, 0, axis_index_groups=X_SETS).reshape(places, tall, span)
    return lax.optimization_barrier((main, rest))


def pick_kernel(rounds, table, gathered, main, rest, spare, info, homes):
    my_z = lax.axis_index("wide") // 8
    my_x = (lax.axis_index("wide") // 2) % 4
    masks = [table[r, 0] & (WIDE - 1) for r in range(rounds)]
    x_masks = [(mask >> 1) & 3 for mask in masks]
    for place in range(MAIN + rounds - CAP):
        homes[place] = -1
    main[...] = jnp.zeros_like(main)
    rest[...] = jnp.zeros_like(rest)
    beyond = jnp.int32(0)
    index = jnp.int32(0)
    places = []
    fresh = []
    for r in range(rounds):
        twin = jnp.int32(-1)
        before = jnp.int32(0)
        for s in range(r):
            twin = jnp.where((masks[s] >> 1) == (masks[r] >> 1), places[s], twin)
            before += jnp.where(x_masks[s] == x_masks[r], fresh[s], 0)
        new = twin < 0
        fits = before < CAP
        place = jnp.where(fits, (my_x ^ x_masks[r]) * CAP + before, MAIN + beyond)
        beyond += jnp.where(new & ~fits, 1, 0)
        over = before - CAP + 1
        moves = new & ~fits & (x_masks[r] != 0)
        index = jnp.where(moves, (x_masks[r] - 1) * (rounds - CAP) + over, index)
        place = jnp.where(new, place, twin)
        places.append(place)
        fresh.append(new.astype(jnp.int32))
        home = my_z ^ (masks[r] >> 3)
        info[r] = masks[r] & 1
        info[rounds + r] = place
        homes[place] = home

        @pl.when(place < MAIN)
        def _():
            main[place] = gathered[home]

        @pl.when(place >= MAIN)
        def _():
            rest[place - MAIN] = gathered[home]

    spare[0] = index


def dot_last(left, right):
    return lax.dot_general(left, right, (((1,), (1,)), ((), ())), preferred_element_type=jnp.float32)


def dot(left, right):
    return jnp.dot(left, right, preferred_element_type=jnp.float32)


def grad_kernel(
    rounds,
    info,
    steepness,
    shift,
    matched,
    shares,
    main,
    rest,
    pictures,
    texts,
    other_pictures,
    other_texts,
    back_main,
    back_rest,
    own,
    left,
):
    rows, span = pictures.shape
    share = main.shape[1] // 2
    first = lax.axis_index("wide") * rows
    begin = lax.axis_index("narrow") * share
    scale = steepness[0] / span
    bias = shift[0]
    lanes = lax.broadcasted_iota(jnp.int32, (share, rows), 1)
    mine = begin + lax.broadcasted_iota(jnp.int32, (share, rows), 0)
    matches = jnp.broadcast_to(matched[...], (share, rows))
    my_match = jnp.sum(jnp.where(lanes == mine, matches, 0), axis=1, keepdims=True)
    back_main[...] = jnp.zeros_like(back_main)
    back_rest[...] = jnp.zeros_like(back_rest)
    for kind in range(2):
        kind_rows = slice(kind * share, (kind + 1) * share)
        left[kind, rounds * share :, :] = shares[kind_rows, :]
        for r in range(rounds):
            place = info[rounds + r]
            left_rows = slice(r * share, (r + 1) * share)

            @pl.when(place < MAIN)
            def _():
                left[kind, left_rows, :] = main[place, kind_rows, :]

            @pl.when(place >= MAIN)
            def _():
                left[kind, left_rows, :] = rest[place - MAIN, kind_rows, :]

    for kind, (block, other) in enumerate([(texts, other_texts), (pictures, other_pictures)]):
        kind_rows = slice(kind * share, (kind + 1) * share)
        near = dot_last(left[kind], block[...])
        far = dot_last(left[kind, : rounds * share, :], other[...])
        near_weights = []
        far_weights = []
        for r in range(rounds):
            apart = info[r] == 1
            left_rows = slice(r * share, (r + 1) * share)
            products = jnp.where(apart, far[left_rows], near[left_rows])
            weights = scale * jax.nn.sigmoid(scale * products + bias)
            near_weights.append(jnp.where(apart, 0.0, weights).astype(jnp.bfloat16))
            far_weights.append(jnp.where(apart, weights, 0.0).astype(jnp.bfloat16))
        same = (my_match == first + lanes) if kind == 0 else (matches == first + mine)
        signs = jnp.where(same, 1.0, -1.0).astype(jnp.float32)
        logits = scale * near[rounds * share :] + bias
        near_weights.append((-scale * signs * jax.nn.sigmoid(-signs * logits)).astype(jnp.bfloat16))
        near_slopes = dot(jnp.concatenate(near_weights, axis=0), block[...])
        slopes = near_slopes[: rounds * share] + dot(jnp.concatenate(far_weights, axis=0), other[...])
        own[kind_rows, :] = near_slopes[rounds * share :]
        for r in range(rounds):
            place = info[rounds + r]
            slope = slopes[r * share : (r + 1) * share]

            @pl.when(place < MAIN)
            def _():
                back_main[place, kind_rows, :] += slope

            @pl.when(place >= MAIN)
            def _():
                back_rest[place - MAIN, kind_rows, :] += slope


def local(
    picture_vectors,
    sentence_vectors,
    matched_text_indices,
    partner_table,
    trained_steepness,
    learned_shift,
):
    rows, span = picture_vectors.shape
    rounds = partner_table.shape[0]
    share = rows // lax.axis_size("narrow")
    begin = lax.axis_index("narrow") * share
    smem = pl.BlockSpec(memory_space=pltpu.SMEM)
    vmem = pl.BlockSpec(memory_space=pltpu.VMEM)

    other_pictures = lax.ppermute(picture_vectors, "wide", xor_pairs(1))
    other_texts = lax.ppermute(sentence_vectors, "wide", xor_pairs(1))
    shares = jnp.concatenate(
        [
            lax.dynamic_slice_in_dim(picture_vectors, begin, share, 0),
            lax.dynamic_slice_in_dim(sentence_vectors, begin, share, 0),
        ],
        axis=0,
    )
    gathered = lax.all_gather(shares, "wide", axis_index_groups=Z_SETS)
    main_shape = (MAIN, 2 * share, span)
    rest_shape = (rounds - CAP, 2 * share, span)
    main, rest, spare, info, homes = pl.pallas_call(
        functools.partial(pick_kernel, rounds),
        out_shape=[
            jax.ShapeDtypeStruct(main_shape, jnp.bfloat16),
            jax.ShapeDtypeStruct(rest_shape, jnp.bfloat16),
            jax.ShapeDtypeStruct((1,), jnp.int32),
            jax.ShapeDtypeStruct((2 * rounds,), jnp.int32),
            jax.ShapeDtypeStruct((MAIN + rounds - CAP,), jnp.int32),
        ],
        in_specs=[smem, vmem],
        out_specs=[vmem, vmem, smem, smem, smem],
        compiler_params=pltpu.CompilerParams(vmem_limit_bytes=PICK_VMEM),
    )(partner_table, gathered)
    main, rest = exchange_x(spare[0], main, rest, False)
    main, rest, own = pl.pallas_call(
        functools.partial(grad_kernel, rounds),
        out_shape=[
            jax.ShapeDtypeStruct(main_shape, jnp.float32),
            jax.ShapeDtypeStruct(rest_shape, jnp.float32),
            jax.ShapeDtypeStruct((2 * share, span), jnp.float32),
        ],
        in_specs=[smem, smem, smem] + [vmem] * 8,
        out_specs=[vmem, vmem, vmem],
        scratch_shapes=[pltpu.VMEM((2, (rounds + 1) * share, span), jnp.bfloat16)],
        compiler_params=pltpu.CompilerParams(vmem_limit_bytes=GRAD_VMEM),
    )(
        info,
        trained_steepness,
        learned_shift,
        matched_text_indices[None, :],
        shares,
        main,
        rest,
        picture_vectors,
        sentence_vectors,
        other_pictures,
        other_texts,
    )
    main, rest = exchange_x(spare[0], main.astype(jnp.float16), rest.astype(jnp.float16), True)
    main, homes = lax.optimization_barrier((main, homes))

    def by_home(stack, places):
        chosen = places[None, :] == jnp.arange(4, dtype=jnp.int32)[:, None]
        return jnp.sum(jnp.where(chosen[:, :, None, None], stack[None].astype(jnp.float32), 0.0), axis=1)

    sums = (by_home(main, homes[:MAIN]) + by_home(rest, homes[MAIN:])).astype(jnp.float16)
    arrived = lax.all_to_all(sums, "wide", 0, 0, axis_index_groups=Z_SETS)
    arrived, own = lax.optimization_barrier((arrived, own))
    slopes = own + jnp.sum(arrived.astype(jnp.float32), axis=0)
    return slopes[:share], slopes[share:]


def solution(mesh):
    in_specs = (P("wide", None), P("wide", None), P("wide"), P(), P(), P())
    out_specs = (P(("wide", "narrow"), None), P(("wide", "narrow"), None))
    return jax.shard_map(local, mesh=mesh, in_specs=in_specs, out_specs=out_specs, check_vma=False)
```

```python
import functools
import jax
import jax.numpy as jnp
from jax import lax
from jax.experimental import pallas as pl
from jax.experimental.pallas import tpu as pltpu
from jax.sharding import PartitionSpec as P

WIDE = 32
Z_SETS = [[low + 8 * z for z in range(4)] for low in range(8)]
X_SETS = [[8 * z + 2 * x + core for x in range(4)] for z in range(4) for core in range(2)]
CAP = 2
MAIN = 4 * CAP
PICK_VMEM = 8 * 1024 * 1024
GRAD_VMEM = 24 * 1024 * 1024


def xor_pairs(mask):
    return [(i, i ^ mask) for i in range(WIDE)]


def move_spare(mask, count, stack):
    moved = lax.ppermute(stack[:count], "wide", xor_pairs(2 * mask))
    return jnp.concatenate([moved, stack[count:]], axis=0) if count < stack.shape[0] else moved


def exchange_x(spare, main, rest, alone):
    places, tall, span = main.shape
    moves = [lambda stack: stack]
    for mask in (1, 2, 3):
        for count in range(1, rest.shape[0] + 1):
            moves.append(functools.partial(move_spare, mask, count))
    rest = lax.switch(spare, moves, rest)
    if alone:
        main, rest = lax.optimization_barrier((main, rest))
    sent = main.reshape(4, CAP * tall, span)
    main = lax.all_to_all(sent, "wide", 0, 0, axis_index_groups=X_SETS).reshape(places, tall, span)
    return lax.optimization_barrier((main, rest))


def pick_kernel(rounds, table, gathered, main, rest, spare, info, homes):
    my_z = lax.axis_index("wide") // 8
    my_x = (lax.axis_index("wide") // 2) % 4
    masks = [table[r, 0] & (WIDE - 1) for r in range(rounds)]
    x_masks = [(mask >> 1) & 3 for mask in masks]
    for place in range(MAIN + rounds - CAP):
        homes[place] = -1
    main[...] = jnp.zeros_like(main)
    rest[...] = jnp.zeros_like(rest)
    beyond = jnp.int32(0)
    index = jnp.int32(0)
    places = []
    fresh = []
    for r in range(rounds):
        twin = jnp.int32(-1)
        before = jnp.int32(0)
        for s in range(r):
            twin = jnp.where((masks[s] >> 1) == (masks[r] >> 1), places[s], twin)
            before += jnp.where(x_masks[s] == x_masks[r], fresh[s], 0)
        new = twin < 0
        fits = before < CAP
        place = jnp.where(fits, (my_x ^ x_masks[r]) * CAP + before, MAIN + beyond)
        beyond += jnp.where(new & ~fits, 1, 0)
        over = before - CAP + 1
        moves = new & ~fits & (x_masks[r] != 0)
        index = jnp.where(moves, (x_masks[r] - 1) * (rounds - CAP) + over, index)
        place = jnp.where(new, place, twin)
        places.append(place)
        fresh.append(new.astype(jnp.int32))
        home = my_z ^ (masks[r] >> 3)
        info[r] = masks[r] & 1
        info[rounds + r] = place
        homes[place] = home

        @pl.when(place < MAIN)
        def _():
            main[place] = gathered[home]

        @pl.when(place >= MAIN)
        def _():
            rest[place - MAIN] = gathered[home]

    spare[0] = index


def dot_last(left, right):
    return lax.dot_general(left, right, (((1,), (1,)), ((), ())), preferred_element_type=jnp.float32)


def dot(left, right):
    return jnp.dot(left, right, preferred_element_type=jnp.float32)


def grad_kernel(
    rounds,
    info,
    steepness,
    shift,
    matched,
    shares,
    main,
    rest,
    pictures,
    texts,
    other_pictures,
    other_texts,
    back_main,
    back_rest,
    own,
    left,
    held,
    sems,
):
    rows, span = pictures.shape
    loads = [
        pltpu.make_async_copy(source, held.at[k], sems.at[k])
        for k, source in enumerate([texts, other_texts, pictures, other_pictures])
    ]
    for load in loads:
        load.start()
    share = main.shape[1] // 2
    first = lax.axis_index("wide") * rows
    begin = lax.axis_index("narrow") * share
    scale = steepness[0] / span
    bias = shift[0]
    lanes = lax.broadcasted_iota(jnp.int32, (share, rows), 1)
    mine = begin + lax.broadcasted_iota(jnp.int32, (share, rows), 0)
    matches = jnp.broadcast_to(matched[...], (share, rows))
    my_match = jnp.sum(jnp.where(lanes == mine, matches, 0), axis=1, keepdims=True)
    back_main[...] = jnp.zeros_like(back_main)
    back_rest[...] = jnp.zeros_like(back_rest)
    for kind in range(2):
        kind_rows = slice(kind * share, (kind + 1) * share)
        left[kind, rounds * share :, :] = shares[kind_rows, :]
        for r in range(rounds):
            place = info[rounds + r]
            left_rows = slice(r * share, (r + 1) * share)

            @pl.when(place < MAIN)
            def _():
                left[kind, left_rows, :] = main[place, kind_rows, :]

            @pl.when(place >= MAIN)
            def _():
                left[kind, left_rows, :] = rest[place - MAIN, kind_rows, :]

    for kind in range(2):
        block, other = held.at[2 * kind], held.at[2 * kind + 1]
        kind_rows = slice(kind * share, (kind + 1) * share)
        loads[2 * kind].wait()
        near = dot_last(left[kind], block[...])
        loads[2 * kind + 1].wait()
        far = dot_last(left[kind, : rounds * share, :], other[...])
        near_weights = []
        far_weights = []
        for r in range(rounds):
            apart = info[r] == 1
            left_rows = slice(r * share, (r + 1) * share)
            products = jnp.where(apart, far[left_rows], near[left_rows])
            weights = scale * jax.nn.sigmoid(scale * products + bias)
            near_weights.append(jnp.where(apart, 0.0, weights).astype(jnp.bfloat16))
            far_weights.append(jnp.where(apart, weights, 0.0).astype(jnp.bfloat16))
        same = (my_match == first + lanes) if kind == 0 else (matches == first + mine)
        signs = jnp.where(same, 1.0, -1.0).astype(jnp.float32)
        logits = scale * near[rounds * share :] + bias
        near_weights.append((-scale * signs * jax.nn.sigmoid(-signs * logits)).astype(jnp.bfloat16))
        near_slopes = dot(jnp.concatenate(near_weights, axis=0), block[...])
        slopes = near_slopes[: rounds * share] + dot(jnp.concatenate(far_weights, axis=0), other[...])
        own[kind_rows, :] = near_slopes[rounds * share :]
        for r in range(rounds):
            place = info[rounds + r]
            slope = slopes[r * share : (r + 1) * share]

            @pl.when(place < MAIN)
            def _():
                back_main[place, kind_rows, :] += slope

            @pl.when(place >= MAIN)
            def _():
                back_rest[place - MAIN, kind_rows, :] += slope


def local(
    picture_vectors,
    sentence_vectors,
    matched_text_indices,
    partner_table,
    trained_steepness,
    learned_shift,
):
    rows, span = picture_vectors.shape
    rounds = partner_table.shape[0]
    share = rows // lax.axis_size("narrow")
    begin = lax.axis_index("narrow") * share
    smem = pl.BlockSpec(memory_space=pltpu.SMEM)
    vmem = pl.BlockSpec(memory_space=pltpu.VMEM)

    other_pictures = lax.ppermute(picture_vectors, "wide", xor_pairs(1))
    other_texts = lax.ppermute(sentence_vectors, "wide", xor_pairs(1))
    shares = jnp.concatenate(
        [
            lax.dynamic_slice_in_dim(picture_vectors, begin, share, 0),
            lax.dynamic_slice_in_dim(sentence_vectors, begin, share, 0),
        ],
        axis=0,
    )
    gathered = lax.all_gather(shares, "wide", axis_index_groups=Z_SETS)
    main_shape = (MAIN, 2 * share, span)
    rest_shape = (rounds - CAP, 2 * share, span)
    main, rest, spare, info, homes = pl.pallas_call(
        functools.partial(pick_kernel, rounds),
        out_shape=[
            jax.ShapeDtypeStruct(main_shape, jnp.bfloat16),
            jax.ShapeDtypeStruct(rest_shape, jnp.bfloat16),
            jax.ShapeDtypeStruct((1,), jnp.int32),
            jax.ShapeDtypeStruct((2 * rounds,), jnp.int32),
            jax.ShapeDtypeStruct((MAIN + rounds - CAP,), jnp.int32),
        ],
        in_specs=[smem, vmem],
        out_specs=[vmem, vmem, smem, smem, smem],
        compiler_params=pltpu.CompilerParams(vmem_limit_bytes=PICK_VMEM),
    )(partner_table, gathered)
    main, rest = exchange_x(spare[0], main, rest, False)
    main, rest, own = pl.pallas_call(
        functools.partial(grad_kernel, rounds),
        out_shape=[
            jax.ShapeDtypeStruct(main_shape, jnp.float32),
            jax.ShapeDtypeStruct(rest_shape, jnp.float32),
            jax.ShapeDtypeStruct((2 * share, span), jnp.float32),
        ],
        in_specs=[smem, smem, smem] + [vmem] * 4 + [pl.BlockSpec(memory_space=pltpu.HBM)] * 4,
        out_specs=[vmem, vmem, vmem],
        scratch_shapes=[
            pltpu.VMEM((2, (rounds + 1) * share, span), jnp.bfloat16),
            pltpu.VMEM((4, rows, span), jnp.bfloat16),
            pltpu.SemaphoreType.DMA((4,)),
        ],
        compiler_params=pltpu.CompilerParams(vmem_limit_bytes=GRAD_VMEM),
    )(
        info,
        trained_steepness,
        learned_shift,
        matched_text_indices[None, :],
        shares,
        main,
        rest,
        *[
            pltpu.with_memory_space_constraint(block, pltpu.HBM)
            for block in (picture_vectors, sentence_vectors, other_pictures, other_texts)
        ],
    )
    main, rest = exchange_x(spare[0], main.astype(jnp.float16), rest.astype(jnp.float16), True)
    main, homes = lax.optimization_barrier((main, homes))

    def by_home(stack, places):
        chosen = places[None, :] == jnp.arange(4, dtype=jnp.int32)[:, None]
        return jnp.sum(jnp.where(chosen[:, :, None, None], stack[None].astype(jnp.float32), 0.0), axis=1)

    sums = (by_home(main, homes[:MAIN]) + by_home(rest, homes[MAIN:])).astype(jnp.float16)
    arrived = lax.all_to_all(sums, "wide", 0, 0, axis_index_groups=Z_SETS)
    arrived, own = lax.optimization_barrier((arrived, own))
    slopes = own + jnp.sum(arrived.astype(jnp.float32), axis=0)
    return slopes[:share], slopes[share:]


def solution(mesh):
    in_specs = (P("wide", None), P("wide", None), P("wide"), P(), P(), P())
    out_specs = (P(("wide", "narrow"), None), P(("wide", "narrow"), None))
    return jax.shard_map(local, mesh=mesh, in_specs=in_specs, out_specs=out_specs, check_vma=False)
```

```python
import functools
import jax
import jax.numpy as jnp
from jax import lax
from jax.experimental import pallas as pl
from jax.experimental.pallas import tpu as pltpu
from jax.sharding import PartitionSpec as P

WIDE = 32
Z_SETS = [[low + 8 * z for z in range(4)] for low in range(8)]
X_SETS = [[8 * z + 2 * x + core for x in range(4)] for z in range(4) for core in range(2)]
CAP = 2
MAIN = 4 * CAP
PICK_VMEM = 8 * 1024 * 1024
GRAD_VMEM = 24 * 1024 * 1024


def xor_pairs(mask):
    return [(i, i ^ mask) for i in range(WIDE)]


def move_spare(mask, count, stack):
    moved = lax.ppermute(stack[:count], "wide", xor_pairs(2 * mask))
    return jnp.concatenate([moved, stack[count:]], axis=0) if count < stack.shape[0] else moved


def exchange_x(spare, main, rest, alone):
    places, tall, span = main.shape
    moves = [lambda stack: stack]
    for mask in (1, 2, 3):
        for count in range(1, rest.shape[0] + 1):
            moves.append(functools.partial(move_spare, mask, count))
    rest = lax.switch(spare, moves, rest)
    if alone:
        main, rest = lax.optimization_barrier((main, rest))
    sent = main.reshape(4, CAP * tall, span)
    main = lax.all_to_all(sent, "wide", 0, 0, axis_index_groups=X_SETS).reshape(places, tall, span)
    return lax.optimization_barrier((main, rest))


def pick_kernel(rounds, partners, gathered, main, rest, spare, info, homes, table, sem):
    load = pltpu.make_async_copy(partners, table, sem)
    load.start()
    main[...] = jnp.zeros_like(main)
    rest[...] = jnp.zeros_like(rest)
    my_z = lax.axis_index("wide") // 8
    my_x = (lax.axis_index("wide") // 2) % 4
    load.wait()
    masks = [table[r, 0] & (WIDE - 1) for r in range(rounds)]
    x_masks = [(mask >> 1) & 3 for mask in masks]
    for place in range(MAIN + rounds - CAP):
        homes[place] = -1
    beyond = jnp.int32(0)
    index = jnp.int32(0)
    places = []
    fresh = []
    for r in range(rounds):
        twin = jnp.int32(-1)
        before = jnp.int32(0)
        for s in range(r):
            twin = jnp.where((masks[s] >> 1) == (masks[r] >> 1), places[s], twin)
            before += jnp.where(x_masks[s] == x_masks[r], fresh[s], 0)
        new = twin < 0
        fits = before < CAP
        place = jnp.where(fits, (my_x ^ x_masks[r]) * CAP + before, MAIN + beyond)
        beyond += jnp.where(new & ~fits, 1, 0)
        over = before - CAP + 1
        moves = new & ~fits & (x_masks[r] != 0)
        index = jnp.where(moves, (x_masks[r] - 1) * (rounds - CAP) + over, index)
        place = jnp.where(new, place, twin)
        places.append(place)
        fresh.append(new.astype(jnp.int32))
        home = my_z ^ (masks[r] >> 3)
        info[r] = masks[r] & 1
        info[rounds + r] = place
        homes[place] = home

        @pl.when(place < MAIN)
        def _():
            main[place] = gathered[home]

        @pl.when(place >= MAIN)
        def _():
            rest[place - MAIN] = gathered[home]

    spare[0] = index


def dot_last(left, right):
    return lax.dot_general(left, right, (((1,), (1,)), ((), ())), preferred_element_type=jnp.float32)


def dot(left, right):
    return jnp.dot(left, right, preferred_element_type=jnp.float32)


def grad_kernel(
    rounds,
    info,
    steepness,
    shift,
    matched,
    shares,
    main,
    rest,
    pictures,
    texts,
    other_pictures,
    other_texts,
    back_main,
    back_rest,
    own,
    left,
    held,
    sems,
):
    rows, span = pictures.shape
    loads = [
        pltpu.make_async_copy(source, held.at[k], sems.at[k])
        for k, source in enumerate([texts, other_texts, pictures, other_pictures])
    ]
    for load in loads:
        load.start()
    share = main.shape[1] // 2
    first = lax.axis_index("wide") * rows
    begin = lax.axis_index("narrow") * share
    scale = steepness[0] / span
    bias = shift[0]
    lanes = lax.broadcasted_iota(jnp.int32, (share, rows), 1)
    mine = begin + lax.broadcasted_iota(jnp.int32, (share, rows), 0)
    matches = jnp.broadcast_to(matched[...], (share, rows))
    my_match = jnp.sum(jnp.where(lanes == mine, matches, 0), axis=1, keepdims=True)
    back_main[...] = jnp.zeros_like(back_main)
    back_rest[...] = jnp.zeros_like(back_rest)
    for kind in range(2):
        kind_rows = slice(kind * share, (kind + 1) * share)
        left[kind, rounds * share :, :] = shares[kind_rows, :]
        for r in range(rounds):
            place = info[rounds + r]
            left_rows = slice(r * share, (r + 1) * share)

            @pl.when(place < MAIN)
            def _():
                left[kind, left_rows, :] = main[place, kind_rows, :]

            @pl.when(place >= MAIN)
            def _():
                left[kind, left_rows, :] = rest[place - MAIN, kind_rows, :]

    for kind in range(2):
        block, other = held.at[2 * kind], held.at[2 * kind + 1]
        kind_rows = slice(kind * share, (kind + 1) * share)
        loads[2 * kind].wait()
        near = dot_last(left[kind], block[...])
        loads[2 * kind + 1].wait()
        far = dot_last(left[kind, : rounds * share, :], other[...])
        near_weights = []
        far_weights = []
        for r in range(rounds):
            apart = info[r] == 1
            left_rows = slice(r * share, (r + 1) * share)
            products = jnp.where(apart, far[left_rows], near[left_rows])
            weights = scale * jax.nn.sigmoid(scale * products + bias)
            near_weights.append(jnp.where(apart, 0.0, weights).astype(jnp.bfloat16))
            far_weights.append(jnp.where(apart, weights, 0.0).astype(jnp.bfloat16))
        same = (my_match == first + lanes) if kind == 0 else (matches == first + mine)
        signs = jnp.where(same, 1.0, -1.0).astype(jnp.float32)
        logits = scale * near[rounds * share :] + bias
        near_weights.append((-scale * signs * jax.nn.sigmoid(-signs * logits)).astype(jnp.bfloat16))
        near_slopes = dot(jnp.concatenate(near_weights, axis=0), block[...])
        slopes = near_slopes[: rounds * share] + dot(jnp.concatenate(far_weights, axis=0), other[...])
        own[kind_rows, :] = near_slopes[rounds * share :]
        for r in range(rounds):
            place = info[rounds + r]
            slope = slopes[r * share : (r + 1) * share]

            @pl.when(place < MAIN)
            def _():
                back_main[place, kind_rows, :] += slope

            @pl.when(place >= MAIN)
            def _():
                back_rest[place - MAIN, kind_rows, :] += slope


def local(
    picture_vectors,
    sentence_vectors,
    matched_text_indices,
    partner_table,
    trained_steepness,
    learned_shift,
):
    rows, span = picture_vectors.shape
    rounds = partner_table.shape[0]
    share = rows // lax.axis_size("narrow")
    begin = lax.axis_index("narrow") * share
    smem = pl.BlockSpec(memory_space=pltpu.SMEM)
    vmem = pl.BlockSpec(memory_space=pltpu.VMEM)

    other_pictures = lax.ppermute(picture_vectors, "wide", xor_pairs(1))
    other_texts = lax.ppermute(sentence_vectors, "wide", xor_pairs(1))
    shares = jnp.concatenate(
        [
            lax.dynamic_slice_in_dim(picture_vectors, begin, share, 0),
            lax.dynamic_slice_in_dim(sentence_vectors, begin, share, 0),
        ],
        axis=0,
    )
    gathered = lax.all_gather(shares, "wide", axis_index_groups=Z_SETS)
    main_shape = (MAIN, 2 * share, span)
    rest_shape = (rounds - CAP, 2 * share, span)
    main, rest, spare, info, homes = pl.pallas_call(
        functools.partial(pick_kernel, rounds),
        out_shape=[
            jax.ShapeDtypeStruct(main_shape, jnp.bfloat16),
            jax.ShapeDtypeStruct(rest_shape, jnp.bfloat16),
            jax.ShapeDtypeStruct((1,), jnp.int32),
            jax.ShapeDtypeStruct((2 * rounds,), jnp.int32),
            jax.ShapeDtypeStruct((MAIN + rounds - CAP,), jnp.int32),
        ],
        in_specs=[pl.BlockSpec(memory_space=pltpu.HBM), vmem],
        out_specs=[vmem, vmem, smem, smem, smem],
        scratch_shapes=[pltpu.SMEM(partner_table.shape, jnp.int32), pltpu.SemaphoreType.DMA],
        compiler_params=pltpu.CompilerParams(vmem_limit_bytes=PICK_VMEM),
    )(pltpu.with_memory_space_constraint(partner_table, pltpu.HBM), gathered)
    main, rest = exchange_x(spare[0], main, rest, False)
    main, rest, own = pl.pallas_call(
        functools.partial(grad_kernel, rounds),
        out_shape=[
            jax.ShapeDtypeStruct(main_shape, jnp.float32),
            jax.ShapeDtypeStruct(rest_shape, jnp.float32),
            jax.ShapeDtypeStruct((2 * share, span), jnp.float32),
        ],
        in_specs=[smem, smem, smem] + [vmem] * 4 + [pl.BlockSpec(memory_space=pltpu.HBM)] * 4,
        out_specs=[vmem, vmem, vmem],
        scratch_shapes=[
            pltpu.VMEM((2, (rounds + 1) * share, span), jnp.bfloat16),
            pltpu.VMEM((4, rows, span), jnp.bfloat16),
            pltpu.SemaphoreType.DMA((4,)),
        ],
        compiler_params=pltpu.CompilerParams(vmem_limit_bytes=GRAD_VMEM),
    )(
        info,
        trained_steepness,
        learned_shift,
        matched_text_indices[None, :],
        shares,
        main,
        rest,
        *[
            pltpu.with_memory_space_constraint(block, pltpu.HBM)
            for block in (picture_vectors, sentence_vectors, other_pictures, other_texts)
        ],
    )
    main, rest = exchange_x(spare[0], main.astype(jnp.float16), rest.astype(jnp.float16), True)
    main, homes = lax.optimization_barrier((main, homes))

    def by_home(stack, places):
        chosen = places[None, :] == jnp.arange(4, dtype=jnp.int32)[:, None]
        return jnp.sum(jnp.where(chosen[:, :, None, None], stack[None].astype(jnp.float32), 0.0), axis=1)

    sums = (by_home(main, homes[:MAIN]) + by_home(rest, homes[MAIN:])).astype(jnp.float16)
    arrived = lax.all_to_all(sums, "wide", 0, 0, axis_index_groups=Z_SETS)
    arrived, own = lax.optimization_barrier((arrived, own))
    slopes = own + jnp.sum(arrived.astype(jnp.float32), axis=0)
    return slopes[:share], slopes[share:]


def solution(mesh):
    in_specs = (P("wide", None), P("wide", None), P("wide"), P(), P(), P())
    out_specs = (P(("wide", "narrow"), None), P(("wide", "narrow"), None))
    return jax.shard_map(local, mesh=mesh, in_specs=in_specs, out_specs=out_specs, check_vma=False)
```
